32 devices in a mesh: sens: 4 (over y, core), tm: 8 (over z, x).
Axes of the slice: x: 2, y: 2, z: 4, core: 2. Of those that a mesh axis runs over, the one named last changes fastest.
Arguments:
- observations: bfloat16 [65536, 2048], P('sens', 'tm'), may hold values from -6 to 6
- loadings: float32 [65536, 128], P('sens'), may hold values from -6 to 6
- noise_var: float32 [65536], P('sens'), may hold values from 0.25 to 4
- decay: float32 [2048, 128], P('tm'), may hold values from 0.4 to 1
- tiles: int32 [3072, 2], replicated, may hold values from 0 to 511, as said below
Outputs:
- new_loadings: float32 [65536, 128], P(('sens', 'tm'))
- new_noise: float32 [65536], P(('sens', 'tm'))
The draws below stay inside these ranges and needn't reach their ends.
Inputs may be any that keep to these rules, and one draw needn't show every extreme that they name: `tiles`: every pair is a distinct tile; every sensor block appears in at least one pair; the second entry is below 8.
All inputs are finite; a program needn't handle non-finite values.
Results may differ from the reference program's by a relative error of at most 0.0059.
Values may be sent and summed in bfloat16 or wider, within the bound.
A program may use at most 128 MiB of HBM per device.

```python
import math
import jax
import jax.numpy as jnp
from jax import lax

FACTORS = 128
BLOCK = 128
WINDOW = 256
SENSORS = 65536
HORIZON_LENGTH = 2048
BLOCKS = 512
WINDOWS = 8
TILES_OBS = 3072


def draw_decay(key, part):
    gradual_seed, quick_seed, extended_seed, perturbation_seed, spike_seed, survival_seed = jax.random.split(key, 6)
    slow_mask = jax.random.uniform(gradual_seed, (FACTORS,)) < 0.5
    fast_rate = jnp.exp(jax.random.uniform(quick_seed, (FACTORS,), jnp.float32, math.log(1.0 / 50.0), math.log(1.0 / 30.0)))
    long_rate = jnp.exp(jax.random.uniform(extended_seed, (FACTORS,), jnp.float32, math.log(0.05 / HORIZON_LENGTH), math.log(0.5 / HORIZON_LENGTH)))
    background_intensity = jnp.where(slow_mask, long_rate, fast_rate)
    stochastic_perturbation = jnp.exp(jax.random.uniform(perturbation_seed, (HORIZON_LENGTH, FACTORS), jnp.float32, -0.35, 0.35))
    spike_occurrences = jax.random.uniform(spike_seed, (HORIZON_LENGTH, 1)) < 3.0 / HORIZON_LENGTH
    surviving_fraction = jax.random.uniform(survival_seed, (HORIZON_LENGTH, FACTORS), jnp.float32, 0.5, 0.8)
    return jnp.exp(-background_intensity[None, :] * stochastic_perturbation) * jnp.where(spike_occurrences, surviving_fraction, 1.0)


def draw_tiles(key, part):
    key_anchor, key_tilt, key_score = jax.random.split(key, 3)
    anchor = jax.random.randint(key_anchor, (BLOCKS,), 0, WINDOWS)
    tilt_bias = jax.random.randint(key_tilt, (BLOCKS,), 0, 4)
    scores = jax.random.randint(key_score, (BLOCKS, WINDOWS), 0, 16) + 8 * tilt_bias[:, None]
    scores = jnp.where(jnp.arange(WINDOWS)[None, :] == anchor[:, None], 1000, scores)
    ranked = scores.reshape(-1) * (BLOCKS * WINDOWS) + jnp.arange(BLOCKS * WINDOWS)
    _, picked = lax.top_k(ranked, TILES_OBS)
    return jnp.stack([picked // WINDOWS, picked % WINDOWS], axis=1).astype(jnp.int32)


def steps_of(rng, dims, pieces, smallest, high):
    level = 1.0
    for axis_at, blocks in pieces:
        steps = jax.random.uniform(jax.random.fold_in(jax.random.fold_in(rng, 6), axis_at), (blocks,), jnp.float32, smallest / len(pieces), high / len(pieces))
        level = level * jnp.repeat(jnp.exp(steps), dims[axis_at] // blocks).reshape((-1,) + (1,) * (len(dims) - 1 - axis_at))
    return level


def centred(stream_key, dims, spread, bound, shards=(), kind=jnp.bfloat16):
    entries = jax.random.normal(stream_key, dims, jnp.float32) * spread
    if len(shards) > 0:
        entries = steps_of(stream_key, dims, shards, -0.22, 0.18) * entries
    return jnp.clip(entries, min=-bound, max=bound).astype(kind)


def setup_inputs(seed: int = 0) -> dict:
    seeds = jax.random.split(jax.random.key(seed), 6)
    observations = centred(seeds[0], (SENSORS, HORIZON_LENGTH), 1.0, 6.0, ((0, 4), (1, 8)))
    loadings = centred(seeds[1], (SENSORS, FACTORS), 1.0, 6.0, ((0, 4),), jnp.float32)
    noise_var = jnp.clip(jnp.exp(math.log(4.0) - 2.7725887 * jax.random.uniform(seeds[2], (SENSORS,), jnp.float32) ** steps_of(seeds[2], (SENSORS,), ((0, 4),), -0.2, 0.2)), 0.25, 4.0)
    decay = draw_decay(jax.random.fold_in(seeds[5], 71), 0)
    tiles = draw_tiles(jax.random.fold_in(seeds[5], 71), 0)
    return {"observations": observations, "loadings": loadings, "noise_var": noise_var, "decay": decay, "tiles": tiles}


HIGH = lax.Precision.HIGHEST

def compose(before_seg, after_seg):
    return (before_seg[0] * after_seg[0], after_seg[0] * before_seg[1] + after_seg[1])

def reference(observations, loadings, noise_var, decay, tiles):
    block_hit = (tiles[:, 0][:, None] == jnp.arange(BLOCKS)[None, :]).astype(jnp.float32)
    window_hit = (tiles[:, 1][:, None] == jnp.arange(WINDOWS)[None, :]).astype(jnp.float32)
    tile_mask = jnp.dot(block_hit.T, window_hit, precision=HIGH)
    counts = jnp.sum(tile_mask, axis=1)
    windowed = observations.reshape(SENSORS, WINDOWS, WINDOW)

    def window_terms(index):
        sensor_mask = jnp.repeat(lax.dynamic_index_in_dim(tile_mask, index, 1, keepdims=False), BLOCK)
        weighted = loadings / noise_var[:, None] * sensor_mask[:, None]
        scaled = weighted.astype(jnp.bfloat16)
        obs_window = lax.dynamic_index_in_dim(windowed, index, 1, keepdims=False)
        info_vec = lax.dot_general(obs_window.astype(jnp.float32), scaled.astype(jnp.float32), (((0,), (0,)), ((), ())), preferred_element_type=jnp.float32)
        information = jnp.dot(weighted.T, loadings, precision=HIGH)
        return (info_vec, information)
    info_all, information_all = lax.map(window_terms, jnp.arange(WINDOWS))
    identity = jnp.eye(FACTORS, dtype=jnp.float32)
    covariance = jnp.linalg.solve(identity[None] + information_all, jnp.broadcast_to(identity, information_all.shape))
    local_est = jnp.einsum('wtk,wkj->wtj', info_all, covariance, precision=HIGH).reshape(HORIZON_LENGTH, FACTORS)
    forward = lax.associative_scan(compose, (decay, local_est), axis=0)[1]
    backward = jnp.flip(lax.associative_scan(compose, (jnp.flip(decay, 0), jnp.flip(local_est, 0)), axis=0)[1], 0)
    smoothed = ((1.0 - decay) / (1.0 + decay) * (forward + backward - local_est)).astype(jnp.bfloat16)
    smooth_win = smoothed.reshape(WINDOWS, WINDOW, FACTORS)
    smooth_wide = smooth_win.astype(jnp.float32)
    moments = jnp.einsum('wtk,wtj->wkj', smooth_wide, smooth_wide, precision=HIGH) + WINDOW * covariance

    def window_cross(totals, index):
        sensor_mask = jnp.repeat(lax.dynamic_index_in_dim(tile_mask, index, 1, keepdims=False), BLOCK)
        obs_window = lax.dynamic_index_in_dim(windowed, index, 1, keepdims=False)
        observed = obs_window * sensor_mask.astype(jnp.bfloat16)[:, None]
        smooth_now = lax.dynamic_index_in_dim(smooth_win, index, 0, keepdims=False)
        cross_terms = totals[0] + jnp.dot(observed.astype(jnp.float32), smooth_now.astype(jnp.float32), preferred_element_type=jnp.float32)
        sums_sq = totals[1] + jnp.sum(jnp.square(observed.astype(jnp.float32)), axis=1)
        return ((cross_terms, sums_sq), None)
    start_totals = (jnp.zeros((SENSORS, FACTORS), jnp.float32), jnp.zeros((SENSORS,), jnp.float32))
    (cross_terms, sums_sq), _ = lax.scan(window_cross, start_totals, jnp.arange(WINDOWS))
    block_moment = jnp.einsum('bw,wij->bij', tile_mask, moments, precision=HIGH)
    cross_blocks = cross_terms.reshape(BLOCKS, BLOCK, FACTORS)
    solved = jnp.linalg.solve(block_moment, jnp.swapaxes(cross_blocks, 1, 2))
    new_loadings = jnp.swapaxes(solved, 1, 2).reshape(SENSORS, FACTORS)
    explained = jnp.sum(new_loadings * cross_terms, axis=1)
    new_noise = (sums_sq - explained) / (WINDOW * jnp.repeat(counts, BLOCK))
    return (new_loadings, new_noise)
```

```python
import functools

import jax
import jax.numpy as jnp
from jax import lax
from jax.experimental import pallas as pl
from jax.experimental.pallas import tpu as pltpu
from jax.sharding import PartitionSpec as P

BLOCK = 128
HIGH = lax.Precision.HIGHEST
F32 = jnp.float32
BF16 = jnp.bfloat16
TILE = 1024


def info_kernel(obs_ref, load_ref, rate_ref, out_ref):
    @pl.when(pl.program_id(0) == 0)
    def _():
        out_ref[...] = jnp.zeros_like(out_ref)

    load = load_ref[...]
    load_hi = load.astype(BF16)
    load_lo = (load - load_hi.astype(F32)).astype(BF16)
    weighted = load.T * rate_ref[...]
    hi = weighted.astype(BF16)
    lo = (weighted - hi.astype(F32)).astype(BF16)
    window = obs_ref.shape[1]
    right = jnp.concatenate([load_hi, load_lo], axis=1)
    factors = load.shape[1]
    out_ref[:, :window] += jnp.dot(hi, obs_ref[...], preferred_element_type=F32)
    both = jnp.dot(hi, right, preferred_element_type=F32)
    out_ref[:, window:] += (
        both[:, :factors] + both[:, factors:] + jnp.dot(lo, load_hi, preferred_element_type=F32)
    )


def info_and_gram(observations, loadings, rate):
    sensors, window = observations.shape
    factors = loadings.shape[1]
    return pl.pallas_call(
        info_kernel,
        grid=(sensors // TILE,),
        in_specs=[
            pl.BlockSpec((TILE, window), lambda i: (i, 0)),
            pl.BlockSpec((TILE, factors), lambda i: (i, 0)),
            pl.BlockSpec((1, TILE), lambda i: (0, i)),
        ],
        out_specs=pl.BlockSpec((factors, window + factors), lambda i: (0, 0)),
        out_shape=jax.ShapeDtypeStruct((factors, window + factors), F32),
        compiler_params=pltpu.CompilerParams(vmem_limit_bytes=40 * 2**20),
    )(observations, loadings, rate)


def invert_in_place(ref, count, size):
    lanes = lax.broadcasted_iota(jnp.int32, (1, size), 1)
    rows = lax.broadcasted_iota(jnp.int32, (size, 1), 0)

    def step(k, carry):
        lane = lanes == k
        sub = rows == k
        for b in range(count):
            a = ref[b]
            row = ref[b, pl.ds(k, 1), :]
            pivot = jnp.sum(jnp.where(lane, row, 0.0), axis=1, keepdims=True)
            scaled = jnp.where(lane, 1.0, row) / pivot
            col = jnp.sum(jnp.where(lane, a, 0.0), axis=1, keepdims=True)
            col = jnp.where(sub, -1.0, col)
            ref[b] = jnp.where(lane | sub, 0.0, a) - col * scaled
        return carry

    lax.fori_loop(0, size, step, 0)


def invert_kernel(a_ref, out_ref):
    out_ref[...] = a_ref[...]
    invert_in_place(out_ref, a_ref.shape[0], a_ref.shape[1])


def invert(a):
    return pl.pallas_call(
        invert_kernel,
        out_shape=jax.ShapeDtypeStruct(a.shape, F32),
        compiler_params=pltpu.CompilerParams(vmem_limit_bytes=40 * 2**20),
    )(a)


def compose(before_seg, after_seg):
    return (before_seg[0] * after_seg[0], after_seg[0] * before_seg[1] + after_seg[1])


def per_device(observations, loadings, noise_var, decay, tiles):
    time_count = lax.axis_size("tm")
    sens_index = lax.axis_index("sens")
    time_index = lax.axis_index("tm")
    sens_dev, window_len = observations.shape
    factors = loadings.shape[1]
    blocks_dev = sens_dev // BLOCK
    blocks_share = blocks_dev // time_count
    block_ids = sens_index * blocks_dev + jnp.arange(blocks_dev)
    block_hit = (tiles[:, 0][:, None] == block_ids[None, :]).astype(BF16)
    window_hit = (tiles[:, 1][:, None] == jnp.arange(time_count)[None, :]).astype(BF16)
    tile_mask = lax.dot_general(
        block_hit, window_hit, (((0,), (0,)), ((), ())), preferred_element_type=F32
    )
    present = lax.dynamic_index_in_dim(tile_mask, time_index, 1, keepdims=False)
    sensor_mask = jnp.repeat(present, BLOCK)
    rate = (sensor_mask / noise_var)[None, :]
    part = info_and_gram(observations, loadings, rate)
    total = lax.psum(part, "sens")
    identity = jnp.eye(factors, dtype=F32)
    covariance = invert((identity + total[:, window_len:])[None])[0]
    local_est = lax.dot_general(
        total[:, :window_len], covariance, (((0,), (0,)), ((), ())), precision=HIGH
    )
    fwd_gain, fwd_local = lax.associative_scan(compose, (decay, local_est), axis=0)
    back_gain, back_local = lax.associative_scan(
        compose, (jnp.flip(decay, 0), jnp.flip(local_est, 0)), axis=0
    )
    back_gain = jnp.flip(back_gain, 0)
    back_local = jnp.flip(back_local, 0)
    mine = jnp.stack([fwd_gain[-1], fwd_local[-1], back_local[0]])
    ends = lax.all_gather(mine, "tm")
    enter_fwd = jnp.zeros((factors,), F32)
    enter_back = jnp.zeros((factors,), F32)
    for w in range(time_count):
        step = ends[w, 0] * enter_fwd + ends[w, 1]
        enter_fwd = jnp.where(w < time_index, step, enter_fwd)
    for w in reversed(range(time_count)):
        step = ends[w, 0] * enter_back + ends[w, 2]
        enter_back = jnp.where(w > time_index, step, enter_back)
    forward = fwd_local + fwd_gain * enter_fwd
    backward = back_local + back_gain * enter_back
    smoothed = ((1.0 - decay) / (1.0 + decay) * (forward + backward - local_est)).astype(BF16)
    mask_mine = lax.dynamic_slice_in_dim(tile_mask, time_index * blocks_share, blocks_share, 0)
    observed = observations * sensor_mask.astype(BF16)[:, None]
    sums_sq = jnp.sum(jnp.square(observed.astype(F32)), axis=1)
    cross_terms = jnp.dot(observed, smoothed, preferred_element_type=F32)
    squares = lax.dot_general(
        smoothed, smoothed, (((0,), (0,)), ((), ())), preferred_element_type=F32
    )
    moment = squares + window_len * covariance
    cross_mine = lax.psum_scatter(cross_terms, "tm", scatter_dimension=0, tiled=True)
    sq_mine = lax.psum_scatter(sums_sq, "tm", scatter_dimension=0, tiled=True)
    all_moments = lax.all_gather(moment[None], "tm", axis=0, tiled=True)
    moment_mine = jnp.einsum("bw,wij->bij", mask_mine, all_moments, precision=HIGH)
    counts_mine = jnp.sum(mask_mine, axis=1)
    inverse = invert(moment_mine)
    cross_blocks = cross_mine.reshape(blocks_share, BLOCK, factors)
    new_loadings = jnp.einsum("bsf,bfg->bsg", cross_blocks, inverse, precision=HIGH).reshape(
        blocks_share * BLOCK, factors
    )
    explained = jnp.sum(new_loadings * cross_mine, axis=1)
    new_noise = (sq_mine - explained) / (window_len * jnp.repeat(counts_mine, BLOCK))
    return (new_loadings, new_noise)


def solution(mesh):
    return jax.shard_map(
        per_device,
        mesh=mesh,
        in_specs=(P("sens", "tm"), P("sens", None), P("sens"), P("tm", None), P()),
        out_specs=(P(("sens", "tm"), None), P(("sens", "tm"))),
        check_vma=False,
    )
```
